32 devices in a mesh: row: 8 (over y, x, core), col: 4 (over z).
Axes of the slice: x: 2, y: 2, z: 4, core: 2. Of those that a mesh axis runs over, the one named last changes fastest.
Arguments:
- delta: float32 [4096, 4096], P('row', 'col'), may hold values from 0.5 to 64, as said below
- coords: float32 [4096, 64], P(('row', 'col')), may hold values from -6 to 6
- block_order: int32 [32], replicated, may hold values from 0 to 31, each once
Outputs:
- embedding: float32 [4096, 64], P(('row', 'col'))
- stress: float32 [4], replicated
The draws below stay inside these ranges and needn't reach their ends.
Inputs may be any that keep to these rules, and one draw needn't show every extreme that they name: `delta`: symmetric, positive off the diagonal. `block_order`: each coordinate block once.
All inputs are finite; a program needn't handle non-finite values.
Results may differ from the reference program's by a relative error of at most 0.0003.
Values sent between devices are 32-bit elements; how exact they have to be, the bound alone decides.
A program may use at most 192 MiB of HBM per device.

```python
import jax
import jax.numpy as jnp
from jax import lax

BLK = 128
DIM = 64
ITERS = 4
BLOCKS = 32
N = 4096
N_ROW = 8
N_COL = 4


def draw_delta(key, part):
    key = jax.random.fold_in(key, 11)
    first_key, second_key = jax.random.split(key)
    position = jnp.arange(N).astype(jnp.float32)
    scales = jnp.exp(jnp.log(3.0) * position / N) * jax.random.uniform(first_key, (N,), jnp.float32, 0.8, 1.25)
    noise = 7.0 + 2.5 * jnp.clip(jax.random.normal(second_key, (N, N), jnp.float32), -2.4, 2.4)
    index = jnp.arange(N).astype(jnp.int32)
    mirrored = jnp.where(index[:, None] <= index[None, :], noise, noise.T)
    return (jnp.sqrt(scales[:, None] * scales[None, :]) * mirrored).astype(jnp.float32)


def block_levels(stream_key, extent, shards, low, top_value):
    factor_of, own = 1.0, jax.random.fold_in(stream_key, 6)
    for dim, parts in shards:
        steps = jnp.exp(jax.random.uniform(jax.random.fold_in(own, dim), (parts,), jnp.float32, low / len(shards), top_value / len(shards)))
        factor_of = factor_of * jnp.repeat(steps, extent[dim] // parts).reshape([-1 if axis == dim else 1 for axis in range(len(extent))])
    return factor_of


def centred(stream_key, extent, spread, reach, cuts=(), kind=jnp.bfloat16):
    loudness = block_levels(stream_key, extent, cuts, -0.22, 0.18) if cuts else 1.0
    entries = jax.random.normal(stream_key, extent, jnp.float32) * spread * loudness
    return jnp.minimum(jnp.maximum(entries, -reach), reach).astype(kind)


def setup_inputs(seed: int = 0) -> dict:
    key_of = jax.random.split(jax.random.key(seed), 4)
    delta = draw_delta(jax.random.fold_in(key_of[3], 71), 0)
    coords = centred(key_of[1], (N, DIM), 1.0, 6.0, ((0, 32),), jnp.float32)
    block_order = jax.random.permutation(key_of[2], BLOCKS).astype(jnp.int32)
    return dict(delta=delta, coords=coords, block_order=block_order)


def tile_update(tile, diagonal, row_coords, col_coords):
    gram = jnp.dot(row_coords, col_coords.T, precision=lax.Precision.HIGHEST, preferred_element_type=jnp.float32)
    row_squares = lax.optimization_barrier(jnp.sum(row_coords * row_coords, axis=1))
    col_squares = lax.optimization_barrier(jnp.sum(col_coords * col_coords, axis=1))
    squared = row_squares[:, None] + col_squares[None, :] - 2.0 * gram
    distance = jnp.sqrt(jnp.where(diagonal, 1.0, squared) + 1e-06)
    ratio = jnp.where(diagonal, 0.0, tile / distance)
    partial_value = lax.optimization_barrier(jnp.sum(ratio, axis=1))[:, None] * row_coords - jnp.dot(ratio, col_coords, precision=lax.Precision.HIGHEST, preferred_element_type=jnp.float32)
    misfit = jnp.sum(jnp.where(diagonal, 0.0, (tile - distance) ** 2))
    return (partial_value, misfit)

def reference(delta, coords, block_order):
    total_points = coords.shape[0]
    block_rows = BLK * N_COL
    ordered = jnp.take(coords.reshape(BLOCKS, BLK, DIM), block_order, axis=0).reshape(total_points, DIM)
    columns = jnp.arange(total_points).astype(jnp.int32)

    def scale_block(index):
        start = (index * block_rows).astype(jnp.int32)
        tile = lax.dynamic_slice_in_dim(delta, start, block_rows, 0)
        diagonal = (start + jnp.arange(block_rows).astype(jnp.int32))[:, None] == columns[None, :]
        return jnp.sum(jnp.where(diagonal, 0.0, tile * tile))
    scale = jnp.sum(lax.map(scale_block, jnp.arange(N_ROW).astype(jnp.int32)))
    current = ordered
    stresses = []
    for iteration in range(ITERS):

        def row_block(index):
            start = (index * block_rows).astype(jnp.int32)
            tile = lax.dynamic_slice_in_dim(delta, start, block_rows, 0)
            row_coords = lax.dynamic_slice_in_dim(current, start, block_rows, 0)
            diagonal = (start + jnp.arange(block_rows).astype(jnp.int32))[:, None] == columns[None, :]
            return tile_update(tile, diagonal, row_coords, current)
        partials, misfits = lax.map(row_block, jnp.arange(N_ROW).astype(jnp.int32))
        stresses.append(jnp.sum(misfits) / scale)
        current = partials.reshape(total_points, DIM) / total_points
    return (current, jnp.stack(stresses).astype(jnp.float32))
```

```python
import functools

import jax
import jax.numpy as jnp
from jax import lax
from jax.experimental import pallas as pl
from jax.experimental.pallas import tpu as pltpu
from jax.sharding import PartitionSpec as P

ITERS = 4
MESH = pl.DeviceIdType.MESH
F32 = jnp.float32
BF16 = jnp.bfloat16
STEP = 256


class Exchange:
    def __init__(self, axis, size, send_sem, recv_sem):
        self.axis, self.size = axis, size
        self.me = lax.axis_index(axis)
        self.send_sem, self.recv_sem = send_sem, recv_sem

    def peer(self, offset):
        return lax.rem(self.me + offset, self.size)

    def copy(self, src, dst, peer, slot):
        return pltpu.make_async_remote_copy(
            src_ref=src,
            dst_ref=dst,
            send_sem=self.send_sem.at[peer],
            recv_sem=self.recv_sem.at[slot],
            device_id={self.axis: peer},
            device_id_type=MESH,
        )

    def start_scatter(self, chunks, landing):
        for offset in range(1, self.size):
            peer = self.peer(offset)
            self.copy(chunks.at[peer], landing.at[self.me], peer, self.me).start()

    def start_gather(self, blocks):
        for offset in range(1, self.size):
            peer = self.peer(offset)
            self.copy(blocks.at[self.me], blocks.at[self.me], peer, self.me).start()

    def wait_recv(self, landing):
        for offset in range(1, self.size):
            peer = self.peer(offset)
            self.copy(landing.at[peer], landing.at[peer], peer, peer).wait_recv()

    def wait_send(self, chunks):
        for offset in range(1, self.size):
            peer = self.peer(offset)
            self.copy(chunks.at[peer], chunks.at[peer], peer, peer).wait_send()


def fold(values):
    rows, cols = values.shape
    tall = jnp.sum(values.reshape(rows // 8, 8, cols), axis=0)
    total = tall[:, :128]
    for start in range(128, cols, 128):
        total = total + tall[:, start : start + 128]
    return total


def split(block):
    high = block.astype(BF16)
    low = (block - high.astype(F32)).astype(BF16)
    return high, low


def kernel(
    n_row,
    n_col,
    order_ref,
    delta_hbm,
    coords_ref,
    out_ref,
    stress_ref,
    delta,
    rat_hi,
    rat_lo,
    left,
    right,
    w_row,
    w_col,
    sq_row,
    sq_col,
    acc_row,
    acc_col,
    chunks_r,
    chunks_c,
    land_r,
    land_c,
    ag_r,
    ag_c,
    fin,
    misfit_acc,
    totals,
    delta_sem,
    sems_r,
    sems_c,
):
    blk, dim = coords_ref.shape
    rows, cols = delta.shape
    points = blk * n_row * n_col
    rs_r = Exchange("col", n_col, sems_r.at[0], sems_r.at[1])
    gt_r = Exchange("col", n_col, sems_r.at[2], sems_r.at[3])
    rs_c = Exchange("row", n_row, sems_c.at[0], sems_c.at[1])
    gt_c = Exchange("row", n_row, sems_c.at[2], sems_c.at[3])
    fn_c = Exchange("row", n_row, sems_c.at[4], sems_c.at[5])
    r, c = rs_c.me, rs_r.me

    load = pltpu.make_async_copy(delta_hbm, delta, delta_sem)
    load.start()

    barrier = pltpu.get_barrier_semaphore()
    for exchange in (rs_r, rs_c):
        for offset in range(1, exchange.size):
            pl.semaphore_signal(
                barrier, inc=1, device_id={exchange.axis: exchange.peer(offset)}, device_id_type=MESH
            )
    own = coords_ref[...].T
    ag_r[c] = own
    ag_c[r, 0:dim] = own
    ag_c[r, dim : dim + 8] = jnp.zeros((8, 128), F32)
    pl.semaphore_wait(barrier, n_row + n_col - 2)

    gt_r.start_gather(ag_r)
    gt_c.start_gather(ag_c)

    load.wait()
    misfit_acc[...] = jnp.zeros((8, 128), F32)
    w_row[2 * dim :] = jnp.ones((16, rows), BF16)
    w_col[2 * dim :] = jnp.ones((16, cols), BF16)

    def scale_step(step, carry):
        at = pl.ds(pl.multiple_of(step * STEP, STEP), STEP)
        tile = delta[:, at]
        row_id = r * rows + lax.broadcasted_iota(jnp.int32, tile.shape, 0)
        col_id = c * cols + step * STEP + lax.broadcasted_iota(jnp.int32, tile.shape, 1)
        tile = jnp.where(row_id == col_id, 0.0, tile)
        delta[:, at] = tile
        misfit_acc[...] += fold(tile * tile)
        return carry

    lax.fori_loop(0, cols // STEP, scale_step, 0)

    gt_r.wait_recv(ag_r)
    gt_c.wait_recv(ag_c)
    gt_r.wait_send(ag_r)
    gt_c.wait_send(ag_c)

    for k in range(n_col):
        stored = order_ref[r * n_col + k]
        here = lax.rem(stored, n_col) == c
        chunks_r[k, 0:dim] = jnp.where(here, ag_c[lax.div(stored, n_col), 0:dim], 0.0)
        chunks_r[k, dim : dim + 8] = misfit_acc[...]
    for k in range(n_row):
        stored = order_ref[c * n_row + k]
        here = lax.div(stored, n_col) == r
        chunks_c[k] = jnp.where(here, ag_r[lax.rem(stored, n_col)], 0.0)
    rs_r.start_scatter(chunks_r, land_r)
    rs_c.start_scatter(chunks_c, land_c)

    def reduced_row(factor):
        rs_r.wait_recv(land_r)
        total = chunks_r[c]
        for offset in range(1, n_col):
            total = total + land_r[rs_r.peer(offset)]
        return total[0:dim] * factor, total[dim : dim + 8]

    def finish(number, factor):
        share, misfit = reduced_row(factor)
        ag_r[c] = share
        gt_r.start_gather(ag_r)
        rs_c.wait_recv(land_c)
        total = chunks_c[r]
        for offset in range(1, n_row):
            total = total + land_c[rs_c.peer(offset)]
        ag_c[r, 0:dim] = total * factor
        ag_c[r, dim : dim + 8] = misfit
        gt_c.start_gather(ag_c)
        rs_r.wait_send(chunks_r)
        rs_c.wait_send(chunks_c)

        gt_r.wait_recv(ag_r)
        for k in range(n_col):
            at = slice(k * blk, (k + 1) * blk)
            high, low = split(ag_r[k])
            w_row[0:dim, at] = high
            w_row[dim : 2 * dim, at] = low
            high, low = high.astype(F32), low.astype(F32)
            kept = high + low
            stacked = jnp.concatenate([high, high, low, low], axis=0) * -2.0
            left[at, :] = stacked.T.astype(BF16)
            sq_row[at, :] = jnp.sum(kept * kept, axis=0, keepdims=True).T
        gt_c.wait_recv(ag_c)
        grand = jnp.zeros((8, 128), F32)
        for k in range(n_row):
            at = slice(k * blk, (k + 1) * blk)
            high, low = split(ag_c[k, 0:dim])
            w_col[0:dim, at] = high
            w_col[dim : 2 * dim, at] = low
            right[0:dim, at] = high
            right[dim : 2 * dim, at] = low
            right[2 * dim : 3 * dim, at] = high
            right[3 * dim : 4 * dim, at] = low
            kept = high.astype(F32) + low.astype(F32)
            sq_col[:, at] = jnp.sum(kept * kept, axis=0, keepdims=True) + 1e-06
            grand = grand + ag_c[k, dim : dim + 8]
        totals[number] = grand
        gt_r.wait_send(ag_r)
        gt_c.wait_send(ag_c)

    def row_sums():
        acc_row[...] = jnp.zeros_like(acc_row)
        misfit_acc[...] = jnp.zeros((8, 128), F32)

        def step_body(step, carry):
            at = pl.ds(pl.multiple_of(step * STEP, STEP), STEP)
            gram = jnp.dot(left[...], right[:, at], preferred_element_type=F32)
            squared = jnp.maximum(sq_row[...] + sq_col[:, at] + gram, 1e-06)
            inverse = lax.rsqrt(squared)
            tile = delta[:, at]
            error = jnp.where(tile > 0.0, tile - squared * inverse, 0.0)
            misfit_acc[...] += fold(error * error)
            high, low = split(tile * inverse)
            rat_hi[:, at] = high
            rat_lo[:, at] = low
            weights = w_col[:, at]
            contract = (((1,), (1,)), ((), ()))
            acc_row[...] += lax.dot_general(
                weights, high, contract, preferred_element_type=F32
            ) + lax.dot_general(weights, low, contract, preferred_element_type=F32)
            return carry

        lax.fori_loop(0, cols // STEP, step_body, 0)
        misfit = misfit_acc[...]
        for k in range(n_col):
            at = slice(k * blk, (k + 1) * blk)
            kept = w_row[0:dim, at].astype(F32) + w_row[dim : 2 * dim, at].astype(F32)
            chunks_r[k, 0:dim] = acc_row[2 * dim : 2 * dim + 1, at] * kept - (
                acc_row[0:dim, at] + acc_row[dim : 2 * dim, at]
            )
            chunks_r[k, dim : dim + 8] = misfit
        rs_r.start_scatter(chunks_r, land_r)

    def col_sums():
        def step_body(step, carry):
            at = pl.ds(pl.multiple_of(step * STEP, STEP), STEP)
            acc_col[:, at] = jnp.dot(
                w_row[...], rat_hi[:, at], preferred_element_type=F32
            ) + jnp.dot(w_row[...], rat_lo[:, at], preferred_element_type=F32)
            return carry

        lax.fori_loop(0, cols // STEP, step_body, 0)
        for k in range(n_row):
            at = slice(k * blk, (k + 1) * blk)
            kept = w_col[0:dim, at].astype(F32) + w_col[dim : 2 * dim, at].astype(F32)
            chunks_c[k] = acc_col[2 * dim : 2 * dim + 1, at] * kept - (
                acc_col[0:dim, at] + acc_col[dim : 2 * dim, at]
            )
        rs_c.start_scatter(chunks_c, land_c)

    finish(0, 1.0)

    def iteration(number, carry):
        row_sums()
        col_sums()
        finish(number, 1.0 / points)
        return carry

    lax.fori_loop(1, ITERS, iteration, 0)
    row_sums()
    share, misfit = reduced_row(1.0 / points)
    fin[r] = misfit
    fn_c.start_gather(fin)
    out_ref[...] = share.T
    rs_r.wait_send(chunks_r)
    fn_c.wait_recv(fin)
    grand = fin[0]
    for k in range(1, n_row):
        grand = grand + fin[k]
    totals[ITERS] = grand
    fn_c.wait_send(fin)
    scale = jnp.sum(totals[0], keepdims=True)
    for number in range(ITERS):
        stress_ref[number] = (jnp.sum(totals[number + 1], keepdims=True) / scale)[0, 0]


def body(n_row, n_col, delta, coords, block_order):
    blk, dim = coords.shape
    rows, cols = delta.shape
    vmem = pl.BlockSpec(memory_space=pltpu.VMEM)
    return pl.pallas_call(
        functools.partial(kernel, n_row, n_col),
        out_shape=(
            jax.ShapeDtypeStruct((blk, dim), F32),
            jax.ShapeDtypeStruct((ITERS,), F32),
        ),
        in_specs=[
            pl.BlockSpec(memory_space=pltpu.SMEM),
            pl.BlockSpec(memory_space=pl.ANY),
            vmem,
        ],
        out_specs=(vmem, pl.BlockSpec(memory_space=pltpu.SMEM)),
        scratch_shapes=[
            pltpu.VMEM((rows, cols), F32),
            pltpu.VMEM((rows, cols), BF16),
            pltpu.VMEM((rows, cols), BF16),
            pltpu.VMEM((rows, 4 * dim), BF16),
            pltpu.VMEM((4 * dim, cols), BF16),
            pltpu.VMEM((2 * dim + 16, rows), BF16),
            pltpu.VMEM((2 * dim + 16, cols), BF16),
            pltpu.VMEM((rows, 1), F32),
            pltpu.VMEM((1, cols), F32),
            pltpu.VMEM((2 * dim + 16, rows), F32),
            pltpu.VMEM((2 * dim + 16, cols), F32),
            pltpu.VMEM((n_col, dim + 8, blk), F32),
            pltpu.VMEM((n_row, dim, blk), F32),
            pltpu.VMEM((n_col, dim + 8, blk), F32),
            pltpu.VMEM((n_row, dim, blk), F32),
            pltpu.VMEM((n_col, dim, blk), F32),
            pltpu.VMEM((n_row, dim + 8, blk), F32),
            pltpu.VMEM((n_row, 8, 128), F32),
            pltpu.VMEM((8, 128), F32),
            pltpu.VMEM((ITERS + 1, 8, 128), F32),
            pltpu.SemaphoreType.DMA,
            pltpu.SemaphoreType.DMA((4, n_col)),
            pltpu.SemaphoreType.DMA((6, n_row)),
        ],
        compiler_params=pltpu.CompilerParams(
            collective_id=0, has_side_effects=True, vmem_limit_bytes=48 * 1024 * 1024
        ),
    )(block_order, delta, coords)


def solution(mesh):
    sizes = dict(mesh.shape)
    return jax.shard_map(
        functools.partial(body, sizes["row"], sizes["col"]),
        mesh=mesh,
        in_specs=(P("row", "col"), P(("row", "col"), None), P()),
        out_specs=(P(("row", "col"), None), P()),
        check_vma=False,
    )
```

```python
import functools

import jax
import jax.numpy as jnp
from jax import lax
from jax.experimental import pallas as pl
from jax.experimental.pallas import tpu as pltpu
from jax.sharding import PartitionSpec as P

ITERS = 4
MESH = pl.DeviceIdType.MESH
F32 = jnp.float32
BF16 = jnp.bfloat16
STEP = 512
UNROLL = False


class Exchange:
    def __init__(self, axis, size, send_sem, recv_sem):
        self.axis, self.size = axis, size
        self.me = lax.axis_index(axis)
        self.send_sem, self.recv_sem = send_sem, recv_sem

    def peer(self, offset):
        return lax.rem(self.me + offset, self.size)

    def copy(self, src, dst, peer, slot):
        return pltpu.make_async_remote_copy(
            src_ref=src,
            dst_ref=dst,
            send_sem=self.send_sem.at[peer],
            recv_sem=self.recv_sem.at[slot],
            device_id={self.axis: peer},
            device_id_type=MESH,
        )

    def start_scatter(self, chunks, landing):
        for offset in range(1, self.size):
            peer = self.peer(offset)
            self.copy(chunks.at[peer], landing.at[self.me], peer, self.me).start()

    def start_gather(self, blocks):
        for offset in range(1, self.size):
            peer = self.peer(offset)
            self.copy(blocks.at[self.me], blocks.at[self.me], peer, self.me).start()

    def wait_recv(self, landing):
        for offset in range(1, self.size):
            peer = self.peer(offset)
            self.copy(landing.at[peer], landing.at[peer], peer, peer).wait_recv()

    def wait_one(self, landing, peer):
        self.copy(landing.at[peer], landing.at[peer], peer, peer).wait_recv()

    def wait_send(self, chunks):
        for offset in range(1, self.size):
            peer = self.peer(offset)
            self.copy(chunks.at[peer], chunks.at[peer], peer, peer).wait_send()


def fold(values):
    rows, cols = values.shape
    tall = jnp.sum(values.reshape(rows // 8, 8, cols), axis=0)
    total = tall[:, :128]
    for start in range(128, cols, 128):
        total = total + tall[:, start : start + 128]
    return total


def split(block):
    high = block.astype(BF16)
    low = (block - high.astype(F32)).astype(BF16)
    return high, low


def kernel(
    n_row,
    n_col,
    order_ref,
    delta_hbm,
    coords_ref,
    out_ref,
    stress_ref,
    delta,
    left,
    right,
    w_row,
    w_col,
    sq_row,
    sq_col,
    acc_row,
    chunks_r,
    chunks_c,
    land_r,
    land_c,
    ag_r,
    ag_c,
    fin_r,
    fin_c,
    misfit_acc,
    scale_acc,
    pool,
    totals,
    delta_sem,
    pool_sem,
    line_sem,
    plane_sem,
    twin_sem,
    sems_r,
    sems_c,
):
    blk, dim = coords_ref.shape
    rows, cols = delta.shape
    points = blk * n_row * n_col
    rs_r = Exchange("col", n_col, sems_r.at[0], sems_r.at[1])
    gt_r = Exchange("col", n_col, sems_r.at[2], sems_r.at[3])
    rs_c = Exchange("row", n_row, sems_c.at[0], sems_c.at[1])
    gt_c = Exchange("row", n_row, sems_c.at[2], sems_c.at[3])
    fn_r = Exchange("col", n_col, sems_r.at[4], sems_r.at[5])
    fn_c = Exchange("row", n_row, sems_c.at[4], sems_c.at[5])
    r, c = rs_c.me, rs_r.me

    load = pltpu.make_async_copy(delta_hbm, delta, delta_sem)
    load.start()

    barrier = pltpu.get_barrier_semaphore()
    for exchange in (rs_r, rs_c):
        for offset in range(1, exchange.size):
            pl.semaphore_signal(
                barrier, inc=1, device_id={exchange.axis: exchange.peer(offset)}, device_id_type=MESH
            )
    twin = r + 1 - 2 * lax.rem(r, 2)
    own = r * n_col + c
    pool[own] = coords_ref[...].T
    pl.semaphore_wait(barrier, n_row + n_col - 2)

    def pass_on(slot, device, sem):
        return pltpu.make_async_remote_copy(
            src_ref=pool.at[slot],
            dst_ref=pool.at[slot],
            send_sem=sem,
            recv_sem=pool_sem.at[slot],
            device_id=device,
            device_id_type=MESH,
        )

    def arrived(slot):
        pass_on(slot, {"row": twin}, twin_sem.at[0, 0]).wait_recv()

    sent = []

    def send_on(*args):
        copy = pass_on(*args)
        copy.start()
        sent.append(copy)

    lines = n_row // 2
    for offset in range(1, n_col):
        send_on(own, {"col": rs_r.peer(offset)}, line_sem.at[offset])

    def spread(offset):
        slot = r * n_col + rs_r.peer(offset)
        for k in range(1, lines):
            send_on(slot, {"row": rs_c.peer(2 * k)}, plane_sem.at[k, offset])
        send_on(slot, {"row": twin}, twin_sem.at[0, offset])

    spread(0)

    load.wait()
    scale_acc[...] = jnp.zeros((8, 128), F32)
    w_row[2 * dim :] = jnp.ones((16, rows), BF16)
    w_col[2 * dim :] = jnp.ones((16, cols), BF16)

    def scale_step(step, carry):
        at = pl.ds(pl.multiple_of(step * STEP, STEP), STEP)
        tile = delta[:, at]
        row_id = r * rows + lax.broadcasted_iota(jnp.int32, tile.shape, 0)
        col_id = c * cols + step * STEP + lax.broadcasted_iota(jnp.int32, tile.shape, 1)
        tile = jnp.where(row_id == col_id, 0.0, tile)
        delta[:, at] = tile
        scale_acc[...] += fold(tile * tile)
        return carry

    lax.fori_loop(0, cols // STEP, scale_step, 0)

    for offset in range(1, n_col):
        arrived(r * n_col + rs_r.peer(offset))
        spread(offset)
    for offset in range(n_col):
        for k in range(1, lines):
            slot = rs_c.peer(2 * k) * n_col + rs_r.peer(offset)
            arrived(slot)
            send_on(slot, {"row": twin}, twin_sem.at[k, offset])
    for offset in range(n_col):
        for k in range(lines):
            arrived(lax.rem(twin + 2 * k, n_row) * n_col + rs_r.peer(offset))

    def prepare_row(k, block):
        at = pl.ds(pl.multiple_of(k * blk, blk), blk)
        high, low = split(block)
        w_row[0:dim, at] = high
        w_row[dim : 2 * dim, at] = low
        high, low = high.astype(F32), low.astype(F32)
        kept = high + low
        stacked = jnp.concatenate([high, high, low, low], axis=0) * -2.0
        left[at, :] = stacked.T.astype(BF16)
        sq_row[at, :] = jnp.sum(kept * kept, axis=0, keepdims=True).T

    def prepare_col(k, block):
        at = pl.ds(pl.multiple_of(k * blk, blk), blk)
        high, low = split(block)
        w_col[0:dim, at] = high
        w_col[dim : 2 * dim, at] = low
        right[0:dim, at] = high
        right[dim : 2 * dim, at] = low
        right[2 * dim : 3 * dim, at] = high
        right[3 * dim : 4 * dim, at] = low
        kept = high.astype(F32) + low.astype(F32)
        sq_col[:, at] = jnp.sum(kept * kept, axis=0, keepdims=True) + 1e-06

    def reduced_row(factor):
        total = chunks_r[c]
        for offset in range(1, n_col):
            rs_r.wait_one(land_r, rs_r.peer(offset))
            total = total + land_r[rs_r.peer(offset)]
        return total[0:dim] * factor, total[dim : dim + 8]

    def finish(number, factor):
        share, misfit = reduced_row(factor)
        ag_r[c] = share
        gt_r.start_gather(ag_r)
        total = chunks_c[r]
        for offset in range(1, n_row):
            rs_c.wait_one(land_c, rs_c.peer(offset))
            total = total + land_c[rs_c.peer(offset)]
        ag_c[r, 0:dim] = total * factor
        ag_c[r, dim : dim + 8] = misfit
        gt_c.start_gather(ag_c)
        rs_r.wait_send(chunks_r)
        rs_c.wait_send(chunks_c)

        prepare_row(c, ag_r[c])
        prepare_col(r, ag_c[r, 0:dim])
        grand = ag_c[r, dim : dim + 8]
        for offset in range(1, n_col):
            peer = gt_r.peer(offset)
            gt_r.wait_one(ag_r, peer)
            prepare_row(peer, ag_r[peer])
        for offset in range(1, n_row):
            peer = gt_c.peer(offset)
            gt_c.wait_one(ag_c, peer)
            prepare_col(peer, ag_c[peer, 0:dim])
            grand = grand + ag_c[peer, dim : dim + 8]
        totals[number] = grand
        gt_r.wait_send(ag_r)
        gt_c.wait_send(ag_c)

    def tile_pass(more):
        acc_row[...] = jnp.zeros_like(acc_row)
        misfit_acc[...] = jnp.zeros((8, 128), F32)

        def add_row(at, high, low):
            contract = (((1,), (1,)), ((), ()))
            acc_row[...] += lax.dot_general(
                w_col[:, at], high, contract, preferred_element_type=F32
            ) + lax.dot_general(w_col[:, at], low, contract, preferred_element_type=F32)

        def late_step(step, carry):
            at = pl.ds(pl.multiple_of(step * STEP, STEP), STEP)
            add_row(at, *split(delta[:, at]))
            return carry

        def step_body(step, carry):
            at = pl.ds(pl.multiple_of(step * STEP, STEP), STEP)
            gram = jnp.dot(left[...], right[:, at], preferred_element_type=F32)
            squared = jnp.maximum(sq_row[...] + sq_col[:, at] + gram, 1e-06)
            inverse = lax.rsqrt(squared)
            tile = delta[:, at]
            error = jnp.where(tile > 0.0, tile - squared * inverse, 0.0)
            misfit_acc[...] += fold(error * error)
            if not more:
                delta[:, at] = tile * inverse
                return carry
            high, low = split(tile * inverse)
            add_row(at, high, low)
            weights = w_col[:, at]
            sums = jnp.dot(w_row[...], high, preferred_element_type=F32) + jnp.dot(
                w_row[...], low, preferred_element_type=F32
            )
            kept = weights[0:dim].astype(F32) + weights[dim : 2 * dim].astype(F32)
            part = sums[2 * dim : 2 * dim + 1] * kept - (sums[0:dim] + sums[dim : 2 * dim])
            for piece in range(STEP // blk):
                k = step * (STEP // blk) + piece
                chunks_c[k] = part[:, piece * blk : (piece + 1) * blk]

                @pl.when(k != r)
                def _():
                    rs_c.copy(chunks_c.at[k], land_c.at[r], k, r).start()

            return carry

        lax.fori_loop(0, cols // STEP, step_body, 0, unroll=UNROLL)
        misfit = misfit_acc[...]
        if not more:
            fin_c[r, 0:4] = misfit[0:4] + misfit[4:8]
            fin_c[r, 4:8] = scale_acc[0:4] + scale_acc[4:8]
            fn_c.start_gather(fin_c)
            lax.fori_loop(0, cols // STEP, late_step, 0, unroll=UNROLL)
        for k in range(n_col):
            at = slice(k * blk, (k + 1) * blk)
            kept = w_row[0:dim, at].astype(F32) + w_row[dim : 2 * dim, at].astype(F32)
            chunks_r[k, 0:dim] = acc_row[2 * dim : 2 * dim + 1, at] * kept - (
                acc_row[0:dim, at] + acc_row[dim : 2 * dim, at]
            )
            chunks_r[k, dim : dim + 8] = misfit
        rs_r.start_scatter(chunks_r, land_r)
        if not more:
            grand = fin_c[r]
            for offset in range(1, n_row):
                fn_c.wait_one(fin_c, fn_c.peer(offset))
                grand = grand + fin_c[fn_c.peer(offset)]
            fin_r[c] = grand
            fn_r.start_gather(fin_r)

    for k in range(n_col):
        prepare_row(k, pool[order_ref[r * n_col + k]])
    for k in range(n_row):
        prepare_col(k, pool[order_ref[c * n_row + k]])
    for copy in sent:
        copy.wait_send()

    def iteration(number, carry):
        tile_pass(True)
        finish(number, 1.0 / points)
        return carry

    lax.fori_loop(0, ITERS - 1, iteration, 0)
    tile_pass(False)
    share, _ = reduced_row(1.0 / points)
    out_ref[...] = share.T
    fn_r.wait_recv(fin_r)
    grand = fin_r[0]
    for k in range(1, n_col):
        grand = grand + fin_r[k]
    rs_r.wait_send(chunks_r)
    fn_r.wait_send(fin_r)
    fn_c.wait_send(fin_c)
    scale = jnp.sum(grand[4:8], keepdims=True)
    for number in range(ITERS):
        misfit = totals[number] if number < ITERS - 1 else grand[0:4]
        stress_ref[number] = (jnp.sum(misfit, keepdims=True) / scale)[0, 0]


def body(n_row, n_col, delta, coords, block_order):
    blk, dim = coords.shape
    rows, cols = delta.shape
    vmem = pl.BlockSpec(memory_space=pltpu.VMEM)
    return pl.pallas_call(
        functools.partial(kernel, n_row, n_col),
        out_shape=(
            jax.ShapeDtypeStruct((blk, dim), F32),
            jax.ShapeDtypeStruct((ITERS,), F32),
        ),
        in_specs=[
            pl.BlockSpec(memory_space=pltpu.SMEM),
            pl.BlockSpec(memory_space=pl.ANY),
            vmem,
        ],
        out_specs=(vmem, pl.BlockSpec(memory_space=pltpu.SMEM)),
        scratch_shapes=[
            pltpu.VMEM((rows, cols), F32),
            pltpu.VMEM((rows, 4 * dim), BF16),
            pltpu.VMEM((4 * dim, cols), BF16),
            pltpu.VMEM((2 * dim + 16, rows), BF16),
            pltpu.VMEM((2 * dim + 16, cols), BF16),
            pltpu.VMEM((rows, 1), F32),
            pltpu.VMEM((1, cols), F32),
            pltpu.VMEM((2 * dim + 16, rows), F32),
            pltpu.VMEM((n_col, dim + 8, blk), F32),
            pltpu.VMEM((n_row, dim, blk), F32),
            pltpu.VMEM((n_col, dim + 8, blk), F32),
            pltpu.VMEM((n_row, dim, blk), F32),
            pltpu.VMEM((n_col, dim, blk), F32),
            pltpu.VMEM((n_row, dim + 8, blk), F32),
            pltpu.VMEM((n_col, 8, 128), F32),
            pltpu.VMEM((n_row, 8, 128), F32),
            pltpu.VMEM((8, 128), F32),
            pltpu.VMEM((8, 128), F32),
            pltpu.VMEM((n_row * n_col, dim, blk), F32),
            pltpu.VMEM((ITERS, 8, 128), F32),
            pltpu.SemaphoreType.DMA,
            pltpu.SemaphoreType.DMA((n_row * n_col,)),
            pltpu.SemaphoreType.DMA((n_col,)),
            pltpu.SemaphoreType.DMA((n_row // 2, n_col)),
            pltpu.SemaphoreType.DMA((n_row // 2, n_col)),
            pltpu.SemaphoreType.DMA((6, n_col)),
            pltpu.SemaphoreType.DMA((6, n_row)),
        ],
        compiler_params=pltpu.CompilerParams(
            collective_id=0, has_side_effects=True, vmem_limit_bytes=48 * 1024 * 1024
        ),
    )(block_order, delta, coords)


def solution(mesh):
    sizes = dict(mesh.shape)
    return jax.shard_map(
        functools.partial(body, sizes["row"], sizes["col"]),
        mesh=mesh,
        in_specs=(P("row", "col"), P(("row", "col"), None), P()),
        out_specs=(P(("row", "col"), None), P()),
        check_vma=False,
    )
```

```python
import functools

import jax
import jax.numpy as jnp
from jax import lax
from jax.experimental import pallas as pl
from jax.experimental.pallas import tpu as pltpu
from jax.sharding import PartitionSpec as P

ITERS = 4
MESH = pl.DeviceIdType.MESH
F32 = jnp.float32
BF16 = jnp.bfloat16
STEP = 512
UNROLL = True


class Exchange:
    def __init__(self, axis, size, send_sem, recv_sem):
        self.axis, self.size = axis, size
        self.me = lax.axis_index(axis)
        self.send_sem, self.recv_sem = send_sem, recv_sem

    def peer(self, offset):
        return lax.rem(self.me + offset, self.size)

    def copy(self, src, dst, peer, slot):
        return pltpu.make_async_remote_copy(
            src_ref=src,
            dst_ref=dst,
            send_sem=self.send_sem.at[peer],
            recv_sem=self.recv_sem.at[slot],
            device_id={self.axis: peer},
            device_id_type=MESH,
        )

    def start_scatter(self, chunks, landing):
        for offset in range(1, self.size):
            peer = self.peer(offset)
            self.copy(chunks.at[peer], landing.at[self.me], peer, self.me).start()

    def start_gather(self, blocks):
        for offset in range(1, self.size):
            peer = self.peer(offset)
            self.copy(blocks.at[self.me], blocks.at[self.me], peer, self.me).start()

    def wait_recv(self, landing):
        for offset in range(1, self.size):
            peer = self.peer(offset)
            self.copy(landing.at[peer], landing.at[peer], peer, peer).wait_recv()

    def wait_one(self, landing, peer):
        self.copy(landing.at[peer], landing.at[peer], peer, peer).wait_recv()

    def wait_send(self, chunks):
        for offset in range(1, self.size):
            peer = self.peer(offset)
            self.copy(chunks.at[peer], chunks.at[peer], peer, peer).wait_send()


def fold(values):
    rows, cols = values.shape
    tall = jnp.sum(values.reshape(rows // 8, 8, cols), axis=0)
    total = tall[:, :128]
    for start in range(128, cols, 128):
        total = total + tall[:, start : start + 128]
    return total


def split(block):
    high = block.astype(BF16)
    low = (block - high.astype(F32)).astype(BF16)
    return high, low


def kernel(
    n_row,
    n_col,
    order_ref,
    delta_hbm,
    coords_ref,
    out_ref,
    stress_ref,
    delta,
    left,
    right,
    w_row,
    w_col,
    sq_row,
    sq_col,
    acc_row,
    chunks_r,
    chunks_c,
    land_r,
    land_c,
    ag_r,
    ag_c,
    fin_r,
    fin_c,
    misfit_acc,
    scale_acc,
    pool,
    totals,
    delta_sem,
    pool_sem,
    line_sem,
    plane_sem,
    twin_sem,
    sems_r,
    sems_c,
):
    blk, dim = coords_ref.shape
    rows, cols = delta.shape
    points = blk * n_row * n_col
    rs_r = Exchange("col", n_col, sems_r.at[0], sems_r.at[1])
    gt_r = Exchange("col", n_col, sems_r.at[2], sems_r.at[3])
    rs_c = Exchange("row", n_row, sems_c.at[0], sems_c.at[1])
    gt_c = Exchange("row", n_row, sems_c.at[2], sems_c.at[3])
    fn_r = Exchange("col", n_col, sems_r.at[4], sems_r.at[5])
    fn_c = Exchange("row", n_row, sems_c.at[4], sems_c.at[5])
    r, c = rs_c.me, rs_r.me

    load = pltpu.make_async_copy(delta_hbm, delta, delta_sem)
    load.start()

    barrier = pltpu.get_barrier_semaphore()
    for exchange in (rs_r, rs_c):
        for offset in range(1, exchange.size):
            pl.semaphore_signal(
                barrier, inc=1, device_id={exchange.axis: exchange.peer(offset)}, device_id_type=MESH
            )
    twin = r + 1 - 2 * lax.rem(r, 2)
    own = r * n_col + c
    pool[own] = coords_ref[...].T
    pl.semaphore_wait(barrier, n_row + n_col - 2)

    def pass_on(slot, device, sem):
        return pltpu.make_async_remote_copy(
            src_ref=pool.at[slot],
            dst_ref=pool.at[slot],
            send_sem=sem,
            recv_sem=pool_sem.at[slot],
            device_id=device,
            device_id_type=MESH,
        )

    def arrived(slot):
        pass_on(slot, {"row": twin}, twin_sem.at[0, 0]).wait_recv()

    sent = []

    def send_on(*args):
        copy = pass_on(*args)
        copy.start()
        sent.append(copy)

    lines = n_row // 2
    for offset in range(1, n_col):
        send_on(own, {"col": rs_r.peer(offset)}, line_sem.at[offset])

    def spread(offset):
        slot = r * n_col + rs_r.peer(offset)
        for k in range(1, lines):
            send_on(slot, {"row": rs_c.peer(2 * k)}, plane_sem.at[k, offset])
        send_on(slot, {"row": twin}, twin_sem.at[0, offset])

    spread(0)

    load.wait()
    scale_acc[...] = jnp.zeros((8, 128), F32)
    w_row[2 * dim :] = jnp.ones((16, rows), BF16)
    w_col[2 * dim :] = jnp.ones((16, cols), BF16)

    def scale_step(step, carry):
        at = pl.ds(pl.multiple_of(step * STEP, STEP), STEP)
        tile = delta[:, at]
        row_id = r * rows + lax.broadcasted_iota(jnp.int32, tile.shape, 0)
        col_id = c * cols + step * STEP + lax.broadcasted_iota(jnp.int32, tile.shape, 1)
        tile = jnp.where(row_id == col_id, 0.0, tile)
        delta[:, at] = tile
        scale_acc[...] += fold(tile * tile)
        return carry

    lax.fori_loop(0, cols // STEP, scale_step, 0)

    for offset in range(1, n_col):
        arrived(r * n_col + rs_r.peer(offset))
        spread(offset)
    for offset in range(n_col):
        for k in range(1, lines):
            slot = rs_c.peer(2 * k) * n_col + rs_r.peer(offset)
            arrived(slot)
            send_on(slot, {"row": twin}, twin_sem.at[k, offset])
    for offset in range(n_col):
        for k in range(lines):
            arrived(lax.rem(twin + 2 * k, n_row) * n_col + rs_r.peer(offset))

    def prepare_row(k, block):
        at = pl.ds(pl.multiple_of(k * blk, blk), blk)
        high, low = split(block)
        w_row[0:dim, at] = high
        w_row[dim : 2 * dim, at] = low
        high, low = high.astype(F32), low.astype(F32)
        kept = high + low
        stacked = jnp.concatenate([high, high, low, low], axis=0) * -2.0
        left[at, :] = stacked.T.astype(BF16)
        sq_row[at, :] = jnp.sum(kept * kept, axis=0, keepdims=True).T

    def prepare_col(k, block):
        at = pl.ds(pl.multiple_of(k * blk, blk), blk)
        high, low = split(block)
        w_col[0:dim, at] = high
        w_col[dim : 2 * dim, at] = low
        right[0:dim, at] = high
        right[dim : 2 * dim, at] = low
        right[2 * dim : 3 * dim, at] = high
        right[3 * dim : 4 * dim, at] = low
        kept = high.astype(F32) + low.astype(F32)
        sq_col[:, at] = jnp.sum(kept * kept, axis=0, keepdims=True) + 1e-06

    def reduced(exchange, chunks, landing, factor):
        total = chunks[exchange.me]
        for offset in range(1, exchange.size):
            peer = exchange.peer(offset)
            exchange.wait_one(landing, peer)
            total = total + landing[peer]
        return total * factor

    def finish(factor):
        ag_c[r] = reduced(rs_c, chunks_c, land_c, factor)
        gt_c.start_gather(ag_c)
        ag_r[c] = reduced(rs_r, chunks_r, land_r, factor)
        gt_r.start_gather(ag_r)
        prepare_col(r, ag_c[r])
        prepare_row(c, ag_r[c])
        rs_r.wait_send(chunks_r)
        rs_c.wait_send(chunks_c)
        for offset in range(1, n_row):
            peer = gt_c.peer(offset)
            gt_c.wait_one(ag_c, peer)
            prepare_col(peer, ag_c[peer])
        for offset in range(1, n_col):
            peer = gt_r.peer(offset)
            gt_r.wait_one(ag_r, peer)
            prepare_row(peer, ag_r[peer])
        gt_r.wait_send(ag_r)
        gt_c.wait_send(ag_c)

    def tile_pass(number, more):
        acc_row[...] = jnp.zeros_like(acc_row)
        misfit_acc[...] = jnp.zeros((8, 128), F32)

        def add_row(at, high, low):
            contract = (((1,), (1,)), ((), ()))
            weights = w_col[:, at]
            acc_row[...] += lax.dot_general(
                jnp.concatenate([weights, weights], axis=1),
                jnp.concatenate([high, low], axis=1),
                contract,
                preferred_element_type=F32,
            )

        def late_step(step, carry):
            at = pl.ds(pl.multiple_of(step * STEP, STEP), STEP)
            add_row(at, *split(delta[:, at]))
            return carry

        def step_body(step, carry):
            at = pl.ds(pl.multiple_of(step * STEP, STEP), STEP)
            gram = jnp.dot(left[...], right[:, at], preferred_element_type=F32)
            squared = jnp.maximum(sq_row[...] + sq_col[:, at] + gram, 1e-06)
            inverse = lax.rsqrt(squared)
            tile = delta[:, at]
            error = jnp.where(tile > 0.0, tile - squared * inverse, 0.0)
            misfit_acc[...] += fold(error * error)
            if not more:
                delta[:, at] = tile * inverse
                return carry
            high, low = split(tile * inverse)
            add_row(at, high, low)
            weights = w_col[:, at]
            sums = jnp.dot(w_row[...], high, preferred_element_type=F32) + jnp.dot(
                w_row[...], low, preferred_element_type=F32
            )
            kept = weights[0:dim].astype(F32) + weights[dim : 2 * dim].astype(F32)
            part = sums[2 * dim : 2 * dim + 1] * kept - (sums[0:dim] + sums[dim : 2 * dim])
            for piece in range(STEP // blk):
                k = step * (STEP // blk) + piece
                chunks_c[k] = part[:, piece * blk : (piece + 1) * blk]

                @pl.when(k != r)
                def _():
                    rs_c.copy(chunks_c.at[k], land_c.at[r], k, r).start()

            return carry

        lax.fori_loop(0, cols // STEP, step_body, 0, unroll=UNROLL)
        misfit = misfit_acc[...]
        if more:
            totals[number] = misfit
        else:
            sums = [jnp.sum(totals[k], axis=0, keepdims=True) for k in range(ITERS - 1)]
            sums += [jnp.sum(misfit, axis=0, keepdims=True)]
            sums += [jnp.sum(scale_acc[...], axis=0, keepdims=True)]
            sums += [jnp.zeros((8 - len(sums), 128), F32)]
            fin_c[r] = jnp.concatenate(sums, axis=0)
            fn_c.start_gather(fin_c)
            lax.fori_loop(0, cols // STEP, late_step, 0, unroll=UNROLL)
        for k in range(n_col):
            at = slice(k * blk, (k + 1) * blk)
            kept = w_row[0:dim, at].astype(F32) + w_row[dim : 2 * dim, at].astype(F32)
            chunks_r[k] = acc_row[2 * dim : 2 * dim + 1, at] * kept - (
                acc_row[0:dim, at] + acc_row[dim : 2 * dim, at]
            )
        rs_r.start_scatter(chunks_r, land_r)
        if not more:
            grand = fin_c[r]
            for offset in range(1, n_row):
                fn_c.wait_one(fin_c, fn_c.peer(offset))
                grand = grand + fin_c[fn_c.peer(offset)]
            fin_r[c] = grand
            fn_r.start_gather(fin_r)

    for k in range(n_col):
        prepare_row(k, pool[order_ref[r * n_col + k]])
    for k in range(n_row):
        prepare_col(k, pool[order_ref[c * n_row + k]])
    for copy in sent:
        copy.wait_send()

    def iteration(number, carry):
        tile_pass(number, True)
        finish(1.0 / points)
        return carry

    lax.fori_loop(0, ITERS - 1, iteration, 0)
    tile_pass(ITERS - 1, False)
    share = reduced(rs_r, chunks_r, land_r, 1.0 / points)
    out_ref[...] = share.T
    fn_r.wait_recv(fin_r)
    grand = fin_r[0]
    for k in range(1, n_col):
        grand = grand + fin_r[k]
    rs_r.wait_send(chunks_r)
    fn_r.wait_send(fin_r)
    fn_c.wait_send(fin_c)
    sums = jnp.sum(grand, axis=1, keepdims=True)
    stress = sums / sums[ITERS : ITERS + 1]
    for number in range(ITERS):
        stress_ref[number] = stress[number, 0]


def body(n_row, n_col, delta, coords, block_order):
    blk, dim = coords.shape
    rows, cols = delta.shape
    vmem = pl.BlockSpec(memory_space=pltpu.VMEM)
    return pl.pallas_call(
        functools.partial(kernel, n_row, n_col),
        out_shape=(
            jax.ShapeDtypeStruct((blk, dim), F32),
            jax.ShapeDtypeStruct((ITERS,), F32),
        ),
        in_specs=[
            pl.BlockSpec(memory_space=pltpu.SMEM),
            pl.BlockSpec(memory_space=pl.ANY),
            vmem,
        ],
        out_specs=(vmem, pl.BlockSpec(memory_space=pltpu.SMEM)),
        scratch_shapes=[
            pltpu.VMEM((rows, cols), F32),
            pltpu.VMEM((rows, 4 * dim), BF16),
            pltpu.VMEM((4 * dim, cols), BF16),
            pltpu.VMEM((2 * dim + 16, rows), BF16),
            pltpu.VMEM((2 * dim + 16, cols), BF16),
            pltpu.VMEM((rows, 1), F32),
            pltpu.VMEM((1, cols), F32),
            pltpu.VMEM((2 * dim + 16, rows), F32),
            pltpu.VMEM((n_col, dim, blk), F32),
            pltpu.VMEM((n_row, dim, blk), F32),
            pltpu.VMEM((n_col, dim, blk), F32),
            pltpu.VMEM((n_row, dim, blk), F32),
            pltpu.VMEM((n_col, dim, blk), F32),
            pltpu.VMEM((n_row, dim, blk), F32),
            pltpu.VMEM((n_col, 8, 128), F32),
            pltpu.VMEM((n_row, 8, 128), F32),
            pltpu.VMEM((8, 128), F32),
            pltpu.VMEM((8, 128), F32),
            pltpu.VMEM((n_row * n_col, dim, blk), F32),
            pltpu.VMEM((ITERS, 8, 128), F32),
            pltpu.SemaphoreType.DMA,
            pltpu.SemaphoreType.DMA((n_row * n_col,)),
            pltpu.SemaphoreType.DMA((n_col,)),
            pltpu.SemaphoreType.DMA((n_row // 2, n_col)),
            pltpu.SemaphoreType.DMA((n_row // 2, n_col)),
            pltpu.SemaphoreType.DMA((6, n_col)),
            pltpu.SemaphoreType.DMA((6, n_row)),
        ],
        compiler_params=pltpu.CompilerParams(
            collective_id=0, has_side_effects=True, vmem_limit_bytes=48 * 1024 * 1024
        ),
    )(block_order, delta, coords)


def solution(mesh):
    sizes = dict(mesh.shape)
    return jax.shard_map(
        functools.partial(body, sizes["row"], sizes["col"]),
        mesh=mesh,
        in_specs=(P("row", "col"), P(("row", "col"), None), P()),
        out_specs=(P(("row", "col"), None), P()),
        check_vma=False,
    )
```

```python
import functools

import jax
import jax.numpy as jnp
from jax import lax
from jax.experimental import pallas as pl
from jax.experimental.pallas import tpu as pltpu
from jax.sharding import PartitionSpec as P

ITERS = 4
MESH = pl.DeviceIdType.MESH
F32 = jnp.float32
BF16 = jnp.bfloat16
STEP = 512
UNROLL = True


class Exchange:
    def __init__(self, axis, size, send_sem, recv_sem):
        self.axis, self.size = axis, size
        self.me = lax.axis_index(axis)
        self.send_sem, self.recv_sem = send_sem, recv_sem

    def peer(self, offset):
        return lax.rem(self.me + offset, self.size)

    def copy(self, src, dst, peer, slot):
        return pltpu.make_async_remote_copy(
            src_ref=src,
            dst_ref=dst,
            send_sem=self.send_sem.at[peer],
            recv_sem=self.recv_sem.at[slot],
            device_id={self.axis: peer},
            device_id_type=MESH,
        )

    def start_scatter(self, chunks, landing):
        for offset in range(1, self.size):
            peer = self.peer(offset)
            self.copy(chunks.at[peer], landing.at[self.me], peer, self.me).start()

    def start_gather(self, blocks):
        for offset in range(1, self.size):
            peer = self.peer(offset)
            self.copy(blocks.at[self.me], blocks.at[self.me], peer, self.me).start()

    def wait_recv(self, landing):
        for offset in range(1, self.size):
            peer = self.peer(offset)
            self.copy(landing.at[peer], landing.at[peer], peer, peer).wait_recv()

    def wait_one(self, landing, peer):
        self.copy(landing.at[peer], landing.at[peer], peer, peer).wait_recv()

    def wait_send(self, chunks):
        for offset in range(1, self.size):
            peer = self.peer(offset)
            self.copy(chunks.at[peer], chunks.at[peer], peer, peer).wait_send()


def fold(values):
    rows, cols = values.shape
    tall = jnp.sum(values.reshape(rows // 8, 8, cols), axis=0)
    total = tall[:, :128]
    for start in range(128, cols, 128):
        total = total + tall[:, start : start + 128]
    return total


def split(block):
    high = block.astype(BF16)
    low = (block - high.astype(F32)).astype(BF16)
    return high, low


def kernel(
    n_row,
    n_col,
    order_ref,
    delta_hbm,
    coords_ref,
    out_ref,
    stress_ref,
    delta,
    left,
    right,
    w_row,
    w_col,
    sq_row,
    sq_col,
    acc_row,
    chunks_r,
    chunks_c,
    land_r,
    land_c,
    ag_r,
    ag_c,
    fin_r,
    fin_c,
    misfit_acc,
    scale_acc,
    pool,
    totals,
    delta_sem,
    pool_sem,
    line_sem,
    plane_sem,
    twin_sem,
    sems_r,
    sems_c,
):
    blk, dim = coords_ref.shape
    rows, cols = delta.shape
    points = blk * n_row * n_col
    rs_r = Exchange("col", n_col, sems_r.at[0], sems_r.at[1])
    gt_r = Exchange("col", n_col, sems_r.at[2], sems_r.at[3])
    rs_c = Exchange("row", n_row, sems_c.at[0], sems_c.at[1])
    gt_c = Exchange("row", n_row, sems_c.at[2], sems_c.at[3])
    fn_r = Exchange("col", n_col, sems_r.at[4], sems_r.at[5])
    fn_c = Exchange("row", n_row, sems_c.at[4], sems_c.at[5])
    r, c = rs_c.me, rs_r.me

    load = pltpu.make_async_copy(delta_hbm, delta, delta_sem)
    load.start()

    barrier = pltpu.get_barrier_semaphore()
    for exchange in (rs_r, rs_c):
        for offset in range(1, exchange.size):
            pl.semaphore_signal(
                barrier, inc=1, device_id={exchange.axis: exchange.peer(offset)}, device_id_type=MESH
            )
    twin = r + 1 - 2 * lax.rem(r, 2)
    own = r * n_col + c
    pool[own] = coords_ref[...].T
    pl.semaphore_wait(barrier, n_row + n_col - 2)

    def pass_on(slot, device, sem):
        return pltpu.make_async_remote_copy(
            src_ref=pool.at[slot],
            dst_ref=pool.at[slot],
            send_sem=sem,
            recv_sem=pool_sem.at[slot],
            device_id=device,
            device_id_type=MESH,
        )

    def arrived(slot):
        pass_on(slot, {"row": twin}, twin_sem.at[0, 0]).wait_recv()

    sent = []

    def send_on(*args):
        copy = pass_on(*args)
        copy.start()
        sent.append(copy)

    lines = n_row // 2
    for offset in range(1, n_col):
        send_on(own, {"col": rs_r.peer(offset)}, line_sem.at[offset])

    def spread(offset):
        slot = r * n_col + rs_r.peer(offset)
        for k in range(1, lines):
            send_on(slot, {"row": rs_c.peer(2 * k)}, plane_sem.at[k, offset])
        send_on(slot, {"row": twin}, twin_sem.at[0, offset])

    spread(0)

    load.wait()
    scale_acc[...] = jnp.zeros((8, 128), F32)
    w_row[2 * dim :] = jnp.ones((16, rows), BF16)
    w_col[2 * dim :] = jnp.ones((16, cols), BF16)

    def scale_step(step, carry):
        at = pl.ds(pl.multiple_of(step * STEP, STEP), STEP)
        tile = delta[:, at]
        row_id = r * rows + lax.broadcasted_iota(jnp.int32, tile.shape, 0)
        col_id = c * cols + step * STEP + lax.broadcasted_iota(jnp.int32, tile.shape, 1)
        tile = jnp.where(row_id == col_id, 0.0, tile)
        delta[:, at] = tile
        scale_acc[...] += fold(tile * tile)
        return carry

    lax.fori_loop(0, cols // STEP, scale_step, 0)

    for offset in range(1, n_col):
        arrived(r * n_col + rs_r.peer(offset))
        spread(offset)
    for offset in range(n_col):
        for k in range(1, lines):
            slot = rs_c.peer(2 * k) * n_col + rs_r.peer(offset)
            arrived(slot)
            send_on(slot, {"row": twin}, twin_sem.at[k, offset])
    for offset in range(n_col):
        for k in range(lines):
            arrived(lax.rem(twin + 2 * k, n_row) * n_col + rs_r.peer(offset))

    def prepare_row(k, block):
        at = pl.ds(pl.multiple_of(k * blk, blk), blk)
        high, low = split(block)
        w_row[0:dim, at] = high
        w_row[dim : 2 * dim, at] = low
        high, low = high.astype(F32), low.astype(F32)
        kept = high + low
        turned = (jnp.concatenate([high, low], axis=0) * -2.0).T.astype(BF16)
        left[at, 0 : 2 * dim] = turned
        left[at, 2 * dim : 4 * dim] = turned
        sq_row[at, :] = jnp.sum(kept * kept, axis=0, keepdims=True).T

    def prepare_col(k, block):
        at = pl.ds(pl.multiple_of(k * blk, blk), blk)
        high, low = split(block)
        w_col[0:dim, at] = high
        w_col[dim : 2 * dim, at] = low
        right[0:dim, at] = high
        right[dim : 2 * dim, at] = high
        right[2 * dim : 3 * dim, at] = low
        right[3 * dim : 4 * dim, at] = low
        kept = high.astype(F32) + low.astype(F32)
        sq_col[:, at] = jnp.sum(kept * kept, axis=0, keepdims=True) + 1e-06

    def reduced(exchange, chunks, landing, factor):
        total = chunks[exchange.me]
        for offset in range(1, exchange.size):
            peer = exchange.peer(offset)
            exchange.wait_one(landing, peer)
            total = total + landing[peer]
        return total * factor

    def finish(factor):
        ag_c[r] = reduced(rs_c, chunks_c, land_c, factor)
        gt_c.start_gather(ag_c)
        ag_r[c] = reduced(rs_r, chunks_r, land_r, factor)
        gt_r.start_gather(ag_r)
        prepare_col(r, ag_c[r])
        prepare_row(c, ag_r[c])
        rs_r.wait_send(chunks_r)
        rs_c.wait_send(chunks_c)
        for offset in range(1, n_row):
            peer = gt_c.peer(offset)
            gt_c.wait_one(ag_c, peer)
            prepare_col(peer, ag_c[peer])
        for offset in range(1, n_col):
            gt_r.wait_one(ag_r, gt_r.peer(offset))
        for offset in range(1, n_col):
            peer = gt_r.peer(offset)
            prepare_row(peer, ag_r[peer])
        gt_r.wait_send(ag_r)
        gt_c.wait_send(ag_c)

    def tile_pass(number, more):
        acc_row[...] = jnp.zeros_like(acc_row)
        misfit_acc[...] = jnp.zeros((8, 128), F32)

        def add_row(at, high, low):
            contract = (((1,), (1,)), ((), ()))
            weights = w_col[:, at]
            acc_row[...] += lax.dot_general(
                jnp.concatenate([weights, weights], axis=1),
                jnp.concatenate([high, low], axis=1),
                contract,
                preferred_element_type=F32,
            )

        def late_step(step, carry):
            at = pl.ds(pl.multiple_of(step * STEP, STEP), STEP)
            add_row(at, *split(delta[:, at]))
            return carry

        def step_body(step, carry):
            at = pl.ds(pl.multiple_of(step * STEP, STEP), STEP)
            gram = jnp.dot(left[...], right[:, at], preferred_element_type=F32)
            squared = jnp.maximum(sq_row[...] + sq_col[:, at] + gram, 1e-06)
            inverse = lax.rsqrt(squared)
            tile = delta[:, at]
            error = jnp.where(tile > 0.0, tile - squared * inverse, 0.0)
            misfit_acc[...] += fold(error * error)
            if not more:
                delta[:, at] = tile * inverse
                return carry
            high, low = split(tile * inverse)
            add_row(at, high, low)
            weights = w_col[:, at]
            sums = jnp.dot(w_row[...], high, preferred_element_type=F32) + jnp.dot(
                w_row[...], low, preferred_element_type=F32
            )
            kept = weights[0:dim].astype(F32) + weights[dim : 2 * dim].astype(F32)
            part = sums[2 * dim : 2 * dim + 1] * kept - (sums[0:dim] + sums[dim : 2 * dim])
            for piece in range(STEP // blk):
                k = step * (STEP // blk) + piece
                chunks_c[k] = part[:, piece * blk : (piece + 1) * blk]

                @pl.when(k != r)
                def _():
                    rs_c.copy(chunks_c.at[k], land_c.at[r], k, r).start()

            return carry

        lax.fori_loop(0, cols // STEP, step_body, 0, unroll=UNROLL)
        misfit = misfit_acc[...]
        if more:
            totals[number] = misfit
        else:
            sums = [jnp.sum(totals[k], axis=0, keepdims=True) for k in range(ITERS - 1)]
            sums += [jnp.sum(misfit, axis=0, keepdims=True)]
            sums += [jnp.sum(scale_acc[...], axis=0, keepdims=True)]
            sums += [jnp.zeros((8 - len(sums), 128), F32)]
            fin_c[r] = jnp.concatenate(sums, axis=0)
            fn_c.start_gather(fin_c)
            lax.fori_loop(0, cols // STEP, late_step, 0, unroll=UNROLL)
        for k in range(n_col):
            at = slice(k * blk, (k + 1) * blk)
            kept = w_row[0:dim, at].astype(F32) + w_row[dim : 2 * dim, at].astype(F32)
            chunks_r[k] = acc_row[2 * dim : 2 * dim + 1, at] * kept - (
                acc_row[0:dim, at] + acc_row[dim : 2 * dim, at]
            )
        rs_r.start_scatter(chunks_r, land_r)
        if not more:
            grand = fin_c[r]
            for offset in range(1, n_row):
                fn_c.wait_one(fin_c, fn_c.peer(offset))
                grand = grand + fin_c[fn_c.peer(offset)]
            fin_r[c] = grand
            fn_r.start_gather(fin_r)

    for k in range(n_col):
        prepare_row(k, pool[order_ref[r * n_col + k]])
    for k in range(n_row):
        prepare_col(k, pool[order_ref[c * n_row + k]])
    for copy in sent:
        copy.wait_send()

    def iteration(number, carry):
        tile_pass(number, True)
        finish(1.0 / points)
        return carry

    lax.fori_loop(0, ITERS - 1, iteration, 0)
    tile_pass(ITERS - 1, False)
    share = reduced(rs_r, chunks_r, land_r, 1.0 / points)
    out_ref[...] = share.T
    fn_r.wait_recv(fin_r)
    grand = fin_r[0]
    for k in range(1, n_col):
        grand = grand + fin_r[k]
    rs_r.wait_send(chunks_r)
    fn_r.wait_send(fin_r)
    fn_c.wait_send(fin_c)
    sums = jnp.sum(grand, axis=1, keepdims=True)
    stress = sums / sums[ITERS : ITERS + 1]
    for number in range(ITERS):
        stress_ref[number] = stress[number, 0]


def body(n_row, n_col, delta, coords, block_order):
    blk, dim = coords.shape
    rows, cols = delta.shape
    vmem = pl.BlockSpec(memory_space=pltpu.VMEM)
    return pl.pallas_call(
        functools.partial(kernel, n_row, n_col),
        out_shape=(
            jax.ShapeDtypeStruct((blk, dim), F32),
            jax.ShapeDtypeStruct((ITERS,), F32),
        ),
        in_specs=[
            pl.BlockSpec(memory_space=pltpu.SMEM),
            pl.BlockSpec(memory_space=pl.ANY),
            vmem,
        ],
        out_specs=(vmem, pl.BlockSpec(memory_space=pltpu.SMEM)),
        scratch_shapes=[
            pltpu.VMEM((rows, cols), F32),
            pltpu.VMEM((rows, 4 * dim), BF16),
            pltpu.VMEM((4 * dim, cols), BF16),
            pltpu.VMEM((2 * dim + 16, rows), BF16),
            pltpu.VMEM((2 * dim + 16, cols), BF16),
            pltpu.VMEM((rows, 1), F32),
            pltpu.VMEM((1, cols), F32),
            pltpu.VMEM((2 * dim + 16, rows), F32),
            pltpu.VMEM((n_col, dim, blk), F32),
            pltpu.VMEM((n_row, dim, blk), F32),
            pltpu.VMEM((n_col, dim, blk), F32),
            pltpu.VMEM((n_row, dim, blk), F32),
            pltpu.VMEM((n_col, dim, blk), F32),
            pltpu.VMEM((n_row, dim, blk), F32),
            pltpu.VMEM((n_col, 8, 128), F32),
            pltpu.VMEM((n_row, 8, 128), F32),
            pltpu.VMEM((8, 128), F32),
            pltpu.VMEM((8, 128), F32),
            pltpu.VMEM((n_row * n_col, dim, blk), F32),
            pltpu.VMEM((ITERS, 8, 128), F32),
            pltpu.SemaphoreType.DMA,
            pltpu.SemaphoreType.DMA((n_row * n_col,)),
            pltpu.SemaphoreType.DMA((n_col,)),
            pltpu.SemaphoreType.DMA((n_row // 2, n_col)),
            pltpu.SemaphoreType.DMA((n_row // 2, n_col)),
            pltpu.SemaphoreType.DMA((6, n_col)),
            pltpu.SemaphoreType.DMA((6, n_row)),
        ],
        compiler_params=pltpu.CompilerParams(
            collective_id=0, has_side_effects=True, vmem_limit_bytes=48 * 1024 * 1024
        ),
    )(block_order, delta, coords)


def solution(mesh):
    sizes = dict(mesh.shape)
    return jax.shard_map(
        functools.partial(body, sizes["row"], sizes["col"]),
        mesh=mesh,
        in_specs=(P("row", "col"), P(("row", "col"), None), P()),
        out_specs=(P(("row", "col"), None), P()),
        check_vma=False,
    )
```
